1024 devices in a mesh: rows: 64 (over y, x), cols: 16 (over z, core).
Axes of the slice: x: 8, y: 8, z: 8, core: 2. Of those that a mesh axis runs over, the one named last changes fastest.
Arguments:
- columns: int32 [2048, 12], P('rows'), may hold values from 0 to 2047, as said below
- fetch: int32 [2048, 12, 12], P('rows'), may hold values from -1 to 11, as said below
- values: bfloat16 [2048, 12, 128, 128], P('rows', None, 'cols'), may hold values from -6 to 6
Outputs:
- new_values: bfloat16 [2048, 12, 128, 128], P('rows', None, 'cols')
The draws below stay inside these ranges and needn't reach their ends.
Inputs may be any that keep to these rules, and one draw needn't show every extreme that they name: Slot 0 of block row i holds column i; the columns of one block row are distinct, and the others are block rows at cyclic distance 1 to 7 from i, modulo 2048. fetch[i, t, s] is the slot u with columns[columns[i, t], u] == columns[i, s], or -1 where there is none.
All inputs are finite; a program needn't handle non-finite values.
Results may differ from the reference program's by a relative error of at most 0.0047.
Values may be sent and summed in bfloat16 or wider, within the bound.
No kernel may reach another device: no remote copies, remote signals or barrier semaphores. Data moves between devices by JAX's collectives and lax.ppermute only.
A program may use at most 64 MiB of HBM per device.

```python
import jax
import jax.numpy as jnp
from jax import lax

BS = 128
K = 12
NB = 2048


def pattern(key):
    reach = (K + 3) // 2
    row_ids = jnp.arange(NB)
    steps_away = jnp.arange(2 * reach)
    distance = jnp.where(steps_away < reach, steps_away + 1, reach - 1 - steps_away)
    candidate = (row_ids[:, None] + distance[None, :]) % NB
    scores = jax.random.randint(key, (NB, 2 * reach), 0, 1 << 20) * (2 * reach) + steps_away[None, :]
    order = jnp.argsort(scores, axis=1)[:, :K - 1]
    others = jnp.take_along_axis(candidate, order, axis=1)
    return jnp.concatenate([row_ids[:, None], others], axis=1).astype(jnp.int32)


def draw_columns(key, part):
    return pattern(key)


def draw_fetch(key, part):
    block_cols = pattern(key)
    other_cols = block_cols[block_cols]
    match = other_cols[:, :, None, :] == block_cols[:, None, :, None]
    slot_ids = jnp.arange(K, dtype=jnp.int32)
    return jnp.max(jnp.where(match, slot_ids, -1), axis=-1).astype(jnp.int32)


def block_levels(stream_key, extent, cuts, least, top_value):
    def one(dim, shards_of):
        heights = jax.random.uniform(jax.random.fold_in(jax.random.fold_in(stream_key, 6), dim), (shards_of,), jnp.float32, least / len(cuts), top_value / len(cuts))
        return jnp.repeat(jnp.exp(heights), extent[dim] // shards_of).reshape((-1,) + (1,) * (len(extent) - dim - 1))

    level = one(*cuts[0])
    for cut in cuts[1:]:
        level = level * one(*cut)
    return level


def bell_draw(rng, shape, deviation, most, pieces=(), kind=jnp.bfloat16):
    values = jax.random.normal(rng, shape, jnp.float32) * deviation
    if len(pieces) > 0:
        values = block_levels(rng, shape, pieces, -0.22, 0.18) * values
    return jnp.clip(values, min=-most, max=most).astype(kind)


def setup_inputs(seed: int = 0) -> dict:
    key_of = jax.random.split(jax.random.key(seed), 4)
    return {
        "columns": draw_columns(jax.random.fold_in(key_of[3], 71), 0),
        "fetch": draw_fetch(jax.random.fold_in(key_of[3], 71), 0),
        "values": bell_draw(key_of[2], (NB, K, BS, BS), 1.0, 6.0, ((0, 64), (2, 16))),
    }


def product(right, left, columns, fetch):
    flat_right = right.reshape(-1, BS, BS)

    def one_row(row):
        cols_row, fetch_row, left_row = row
        pick_index = (cols_row[:, None] * K + jnp.maximum(fetch_row, 0)).astype(jnp.int32)
        picked = jnp.take(flat_right, pick_index.reshape(-1), axis=0).reshape(K, K, BS, BS).astype(jnp.float32)
        picked = jnp.where((fetch_row >= 0)[:, :, None, None], picked, jnp.float32(0.0))
        return jnp.einsum("tswm,tmr->swr", picked, left_row.astype(jnp.float32))

    return lax.map(one_row, (columns, fetch, left))


def reference(columns, fetch, values):
    squared = product(values, values, columns, fetch) / (K * BS)
    identity = jnp.eye(BS, dtype=jnp.float32)
    first_slot = (jnp.arange(K) == 0).astype(jnp.float32)
    shifted = (3.0 * first_slot[None, :, None, None] * identity[None, None] - squared).astype(jnp.bfloat16)
    return (0.5 * product(shifted, values, columns, fetch)).astype(jnp.bfloat16)
```

```python
import functools

import jax
import jax.numpy as jnp
from jax import lax
from jax.experimental import pallas as pl
from jax.experimental.pallas import tpu as pltpu
from jax.sharding import PartitionSpec as P

GROUP = 4


def product_kernel(chunks, is_first, scale, where_ref, index_ref, *refs):
    parts = refs[:4]
    pieces = [refs[4 + 9 * k:13 + 9 * k] for k in range(chunks)]
    rest = refs[4 + 9 * chunks:]
    outs, (window, left, window_sem, left_sem) = rest[:-4], rest[-4:]
    slots, width, size = parts[0].shape[1:]
    ring = size // width
    z, core = where_ref[0], where_ref[1]

    window_copies = []
    for k, part in enumerate(parts):
        window_copies.append(pltpu.make_async_copy(part, window.at[pl.ds(8 * k, 8), pl.ds(0, slots)], window_sem.at[k]))
    left_copies = []
    for g in range(2 * chunks):
        chunk, half = divmod(g, 2)
        group_copies = []
        for k in range(ring):
            away = (0, -1, -2, -3, 1, 2, 3, 4)[k]
            source = pieces[chunk][8] if k == 7 and half == 1 else pieces[chunk][k]
            rows = pl.ds(0 if k == 7 else GROUP * half, GROUP)
            slot = lax.rem(z + away + ring, ring)
            group_copies.append(
                pltpu.make_async_copy(source.at[rows], left.at[pl.ds(GROUP * g, GROUP), :, slot], left_sem.at[g, k])
            )
        left_copies.append(group_copies)
    for copy in window_copies:
        copy.start()
    for group_copies in left_copies:
        for copy in group_copies:
            copy.start()
    window[32, 0] = jnp.zeros((width, size), window.dtype)
    tile_at = window.reshape(window.shape[0] * window.shape[1], width, size)
    for copy in window_copies:
        copy.wait()

    def one_row(i, carry):
        total = jnp.zeros((slots * width, size), jnp.float32)
        base = i * (slots * slots)
        for t in range(0, slots, 2):
            columns = []
            for u in (t, t + 1):
                tiles = []
                for s in range(slots):
                    tiles.append(tile_at[index_ref[base + u * slots + s]])
                columns.append(jnp.concatenate(tiles, axis=0))
            picked = jnp.concatenate(columns, axis=1)
            blocks = left[i, pl.ds(t, 2)].reshape(2 * size, size)
            total += jnp.dot(picked, blocks, preferred_element_type=jnp.float32)
        total = (total * scale).reshape(slots, width, size)
        if is_first:
            (out,) = outs
            out[i] = (-total).astype(out.dtype)
            line = lax.broadcasted_iota(jnp.int32, (width, size), 0)
            lane = lax.broadcasted_iota(jnp.int32, (width, size), 1)
            diagonal = jnp.where(lane == line + z * width, 3.0, 0.0)
            out[i, 0] = (diagonal - total[0]).astype(out.dtype)
        else:
            keep, send = outs
            low, high = total[:, :width // 2], total[:, width // 2:]
            to = lax.rem(i + 8 * core, 16)
            keep[to] = jnp.where(core == 0, low, high).astype(keep.dtype)
            send[to] = jnp.where(core == 0, high, low).astype(send.dtype)
        return carry

    for g in range(2 * chunks):
        for copy in left_copies[g]:
            copy.wait()
        lax.fori_loop(GROUP * g, GROUP * (g + 1), one_row, 0)


def product(is_first, scale, where, index, parts, streams):
    chunks = len(streams)
    slots, width, size = parts[0].shape[1:]
    rows = 8 * chunks
    dtype = parts[0].dtype
    if is_first:
        outs = jax.ShapeDtypeStruct((rows, slots, width, size), dtype)
        out_specs = pl.BlockSpec(memory_space=pltpu.VMEM)
    else:
        outs = [jax.ShapeDtypeStruct((rows, slots, width // 2, size), dtype)] * 2
        out_specs = [pl.BlockSpec(memory_space=pltpu.VMEM)] * 2
    operands = list(parts) + [piece for stream in streams for piece in stream]
    flops = 2 * rows * slots * slots * width * size * size
    return pl.pallas_call(
        functools.partial(product_kernel, chunks, is_first, scale),
        out_shape=outs,
        in_specs=[pl.BlockSpec(memory_space=pltpu.SMEM)] * 2 + [pl.BlockSpec(memory_space=pl.ANY)] * len(operands),
        out_specs=out_specs,
        scratch_shapes=[
            pltpu.VMEM((33, 16, width, size), dtype),
            pltpu.VMEM((rows, slots, size // width, width, size), dtype),
            pltpu.SemaphoreType.DMA((4,)),
            pltpu.SemaphoreType.DMA((2 * chunks, size // width)),
        ],
        compiler_params=pltpu.CompilerParams(vmem_limit_bytes=32 * 2**20),
        cost_estimate=pl.CostEstimate(flops=flops, bytes_accessed=rows * slots * size * size * 2, transcendentals=0),
    )(where, index, *operands)


def gather_ring(streams, ring):
    count = 2 * ring
    up = [(i, (i + 2) % count) for i in range(count)]
    down = [((i + 2) % count, i) for i in range(count)]
    risen = [[piece] for piece in streams]
    fallen = [[piece] for piece in streams]
    for step in range(ring // 2 - 1):
        for k in range(len(streams)):
            risen[k].append(lax.ppermute(risen[k][-1], "cols", up))
            fallen[k].append(lax.ppermute(fallen[k][-1], "cols", down))
    gathered = []
    for k in range(len(streams)):
        half = streams[k].shape[0] // 2
        last_up = lax.ppermute(risen[k][-1][:half], "cols", up)
        last_down = lax.ppermute(fallen[k][-1][half:], "cols", down)
        gathered.append(risen[k] + fallen[k][1:] + [last_up, last_down])
    return gathered


def local(columns, fetch, values):
    rows_here, slots, half_width, size = values.shape
    cols = lax.axis_size("cols")
    count = lax.axis_size("rows")
    col = lax.axis_index("cols")
    z, core = col // 2, col % 2
    first = core == 0
    swap = [(i, i ^ 1) for i in range(cols)]

    def outward(piece):
        pairs = []
        for r in range(count):
            for c in range(cols):
                to = ((r - 1) % count, c + 1) if c % 2 == 0 else ((r + 1) % count, c - 1)
                pairs.append((r * cols + c, to[0] * cols + to[1]))
        return lax.ppermute(piece, ("rows", "cols"), pairs)

    other = lax.ppermute(values, "cols", swap)

    def block(number_first, number_second):
        start = jnp.where(first, 8 * number_first, 8 * number_second)
        mine = lax.dynamic_slice_in_dim(values, start, 8, 0)
        theirs = lax.dynamic_slice_in_dim(other, start, 8, 0)
        low = jnp.where(first, mine, theirs)
        high = jnp.where(first, theirs, mine)
        return jnp.concatenate([low, high], axis=2)

    outer_rows, inner_rows, beyond = block(0, 3), block(1, 2), block(2, 1)
    streams = gather_ring([outer_rows, inner_rows], cols // 2)

    origin = lax.axis_index("rows") * rows_here + core * 16
    total = rows_here * count
    away = (columns - origin + total // 2) % total - total // 2 + 8
    part = jnp.where(first, away // 8, 3 - away // 8)
    place = (part * 8 + away % 8) * 16
    index = jnp.where(fetch >= 0, place[:, :, None] + fetch, 32 * 16)
    index = index.reshape(4, -1)
    index = jnp.where(first, index[:2], index[:1:-1])
    where = jnp.stack([z, core]).astype(jnp.int32)

    scale = 1.0 / (slots * size)
    window = (outward(outer_rows), outer_rows, inner_rows, beyond)
    shifted_outer = product(True, scale, where, index[0], window, streams[:1])
    shifted_outward = outward(shifted_outer)
    shifted_inner = product(True, scale, where, index[1], window, streams[1:])
    shifted_beyond = lax.ppermute(shifted_inner, "cols", swap)
    window = (shifted_outward, shifted_outer, shifted_inner, shifted_beyond)
    keep, send = product(False, 0.5, where, index.reshape(-1), window, streams)
    got = lax.ppermute(send, "cols", swap)
    return jnp.where(first, jnp.concatenate([keep, got]), jnp.concatenate([got, keep]))


def solution(mesh):
    in_specs = (P("rows", None), P("rows", None, None), P("rows", None, "cols", None))
    out_specs = P("rows", None, "cols", None)
    return jax.shard_map(local, mesh=mesh, in_specs=in_specs, out_specs=out_specs, check_vma=False)
```

```python
import functools

import jax
import jax.numpy as jnp
from jax import lax
from jax.experimental import pallas as pl
from jax.experimental.pallas import tpu as pltpu
from jax.sharding import PartitionSpec as P

GROUP = 4
COST = 10


def product_kernel(first_block, is_first, scale, extra, where_ref, index_ref, *refs):
    parts, pieces = refs[:3], refs[3:12]
    outs, (window, left, window_sem, left_sem) = refs[12 + extra:-4], refs[-4:]
    rows, slots, width, size = parts[0].shape
    ring = size // width
    z, core = where_ref[0], where_ref[1]
    first_row = rows * where_ref[2 + first_block]

    window_copies = []
    for k, part in enumerate(parts):
        to = window.at[pl.ds(rows * (first_block + k), rows), pl.ds(0, slots)]
        window_copies.append(pltpu.make_async_copy(part, to, window_sem.at[k]))
    left_copies = []
    for g in range(2):
        group_copies = []
        for k in range(ring):
            away = (0, -1, -2, -3, 1, 2, 3, 4)[k]
            source = pieces[8] if k == 7 and g == 1 else pieces[k]
            from_rows = pl.ds(0 if k == 7 else GROUP * g, GROUP)
            slot = lax.rem(z + away + ring, ring)
            to = left.at[pl.ds(GROUP * g, GROUP), :, slot]
            group_copies.append(pltpu.make_async_copy(source.at[from_rows], to, left_sem.at[g, k]))
        left_copies.append(group_copies)
    for copy in window_copies + left_copies[0] + left_copies[1]:
        copy.start()
    window[4 * rows, 0] = jnp.zeros((width, size), window.dtype)
    tile_at = window.reshape(window.shape[0] * window.shape[1], width, size)
    for copy in window_copies:
        copy.wait()

    def one_row(i, carry):
        total = jnp.zeros((slots * width, size), jnp.float32)
        for t in range(0, slots, 2):
            columns = []
            for u in (t, t + 1):
                tiles = [tile_at[lax.shift_right_logical(index_ref[u % 4, s, first_row + i], 10 * (u // 4)) & 1023] for s in range(slots)]
                columns.append(jnp.concatenate(tiles, axis=0))
            picked = jnp.concatenate(columns, axis=1)
            blocks = left[i, pl.ds(t, 2)].reshape(2 * size, size)
            total += jnp.dot(picked, blocks, preferred_element_type=jnp.float32)
        total = (total * scale).reshape(slots, width, size)
        if is_first:
            (out,) = outs
            out[i] = (-total).astype(out.dtype)
            line = lax.broadcasted_iota(jnp.int32, (width, size), 0)
            lane = lax.broadcasted_iota(jnp.int32, (width, size), 1)
            diagonal = jnp.where(lane == line + z * width, 3.0, 0.0)
            out[i, 0] = (diagonal - total[0]).astype(out.dtype)
        else:
            keep, send = outs
            low, high = total[:, :width // 2], total[:, width // 2:]
            keep[i] = jnp.where(core == 0, low, high).astype(keep.dtype)
            send[i] = jnp.where(core == 0, high, low).astype(send.dtype)
        return carry

    for g in range(2):
        for copy in left_copies[g]:
            copy.wait()
        lax.fori_loop(GROUP * g, GROUP * (g + 1), one_row, 0, unroll=GROUP)


def product(first_block, is_first, scale, where, index, parts, pieces, after=()):
    rows, slots, width, size = parts[0].shape
    dtype = parts[0].dtype
    if is_first:
        outs = jax.ShapeDtypeStruct((rows, slots, width, size), dtype)
        out_specs = pl.BlockSpec(memory_space=pltpu.VMEM)
    else:
        outs = [jax.ShapeDtypeStruct((rows, slots, width // 2, size), dtype)] * 2
        out_specs = [pl.BlockSpec(memory_space=pltpu.VMEM)] * 2
    flops = 2 * rows * slots * slots * width * size * size
    return pl.pallas_call(
        functools.partial(product_kernel, first_block, is_first, scale, len(after)),
        out_shape=outs,
        in_specs=[pl.BlockSpec(memory_space=pltpu.SMEM)] * 2 + [pl.BlockSpec(memory_space=pl.ANY)] * (12 + len(after)),
        out_specs=out_specs,
        scratch_shapes=[
            pltpu.VMEM((4 * rows + 1, 16, width, size), dtype),
            pltpu.VMEM((rows, slots, size // width, width, size), dtype),
            pltpu.SemaphoreType.DMA((3,)),
            pltpu.SemaphoreType.DMA((2, size // width)),
        ],
        compiler_params=pltpu.CompilerParams(vmem_limit_bytes=12 * 2**20),
        cost_estimate=pl.CostEstimate(flops=COST * flops, bytes_accessed=rows * slots * size * size * 2, transcendentals=0),
    )(where, index, *parts, *pieces, *after)


def gather_ring(streams, ring):
    count = 2 * ring
    up = [(i, (i + 2) % count) for i in range(count)]
    down = [((i + 2) % count, i) for i in range(count)]
    risen = [[piece] for piece in streams]
    fallen = [[piece] for piece in streams]
    for step in range(ring // 2 - 1):
        for k in range(len(streams)):
            risen[k].append(lax.ppermute(risen[k][-1], "cols", up))
            fallen[k].append(lax.ppermute(fallen[k][-1], "cols", down))
    gathered = []
    for k in range(len(streams)):
        half = streams[k].shape[0] // 2
        last_up = lax.ppermute(risen[k][-1][:half], "cols", up)
        last_down = lax.ppermute(fallen[k][-1][half:], "cols", down)
        gathered.append(risen[k] + fallen[k][1:] + [last_up, last_down])
    return gathered


def local(columns, fetch, values):
    rows_here, slots, half_width, size = values.shape
    cols = lax.axis_size("cols")
    count = lax.axis_size("rows")
    col = lax.axis_index("cols")
    z, core = col // 2, col % 2
    first = core == 0
    swap = [(i, i ^ 1) for i in range(cols)]

    def outward(piece):
        pairs = []
        for r in range(count):
            for c in range(cols):
                to = ((r - 1) % count, c + 1) if c % 2 == 0 else ((r + 1) % count, c - 1)
                pairs.append((r * cols + c, to[0] * cols + to[1]))
        return lax.ppermute(piece, ("rows", "cols"), pairs)

    other = lax.ppermute(values, "cols", swap)

    def joined(number):
        start = jnp.where(first, 8 * number, 24 - 8 * number)
        mine = lax.dynamic_slice_in_dim(values, start, 8, 0)
        theirs = lax.dynamic_slice_in_dim(other, start, 8, 0)
        low = jnp.where(first, mine, theirs)
        high = jnp.where(first, theirs, mine)
        return jnp.concatenate([low, high], axis=2)

    outer_rows, inner_rows, beyond = joined(0), joined(1), joined(2)
    outer_pieces, inner_pieces = gather_ring([outer_rows, inner_rows], cols // 2)

    origin = lax.axis_index("rows") * rows_here + core * 16
    total = rows_here * count
    away = (columns - origin + total // 2) % total - total // 2 + 8
    part = jnp.where(first, away // 8, 3 - away // 8)
    place = (part * 8 + away % 8) * 16
    index = jnp.where(fetch >= 0, place[:, :, None] + fetch, 32 * 16).transpose(1, 2, 0)
    index = index[:4] + index[4:8] * 1024 + index[8:] * 1024**2
    where = jnp.stack([z, core, 3 * core, 1 + core]).astype(jnp.int32)

    scale = 1.0 / (slots * size)
    shifted_outer = product(0, True, scale, where, index, (outward(outer_rows), outer_rows, inner_rows), outer_pieces)
    shifted_outward = outward(shifted_outer)
    shifted_inner = product(1, True, scale, where, index, (outer_rows, inner_rows, beyond), inner_pieces, [shifted_outer])
    shifted_beyond = lax.ppermute(shifted_inner, "cols", swap)
    keep_outer, send_outer = product(
        0, False, 0.5, where, index, (shifted_outward, shifted_outer, shifted_inner), outer_pieces
    )
    got_outer = lax.ppermute(send_outer, "cols", swap)
    keep_inner, send_inner = product(
        1, False, 0.5, where, index, (shifted_outer, shifted_inner, shifted_beyond), inner_pieces, [keep_outer]
    )
    got_inner = lax.ppermute(send_inner, "cols", swap)
    for_first = jnp.concatenate([keep_outer, keep_inner, got_inner, got_outer])
    for_second = jnp.concatenate([got_outer, got_inner, keep_inner, keep_outer])
    return jnp.where(first, for_first, for_second)


def solution(mesh):
    in_specs = (P("rows", None), P("rows", None, None), P("rows", None, "cols", None))
    out_specs = P("rows", None, "cols", None)
    return jax.shard_map(local, mesh=mesh, in_specs=in_specs, out_specs=out_specs, check_vma=False)
```

```python
import functools

import jax
import jax.numpy as jnp
from jax import lax
from jax.experimental import pallas as pl
from jax.experimental.pallas import tpu as pltpu
from jax.sharding import PartitionSpec as P

GROUP = 4
COST = 10


def product_kernel(first_block, is_first, scale, extra, index_from, *refs):
    parts, pieces = refs[:3], refs[3:12]
    outs, (window, index_ref, index_sem) = refs[12 + extra:-3], refs[-3:]
    rows, slots, width, size = parts[0].shape
    col = lax.axis_index("cols")
    z, core = col // 2, lax.rem(col, 2)
    first_row = rows * jnp.where(core == 0, first_block, 3 - first_block)

    index_copy = pltpu.make_async_copy(index_from, index_ref, index_sem)
    index_copy.start()
    turn = lax.rem(size - width * z, size)
    for k, part in enumerate(parts):
        for row in range(rows):
            window[rows * (first_block + k) + row, pl.ds(0, slots)] = pltpu.roll(part[row], turn, 2)
    window[4 * rows, 0] = jnp.zeros((width, size), window.dtype)
    index_copy.wait()
    tile_at = window.reshape(window.shape[0] * window.shape[1], width, size)

    offset = 0
    if extra == 2:
        offset = rows * (1 - core)
        for out, done in zip(outs, refs[12:14]):
            out[pl.ds(rows - offset, rows)] = done[...]

    def one_row(half, i, carry):
        total = jnp.zeros((slots * width, size), jnp.float32)
        for t in range(0, slots, 2):
            columns, blocks = [], []
            for u in (t, t + 1):
                tiles = []
                for s in range(slots):
                    word = index_ref[u % 4, s, first_row + i]
                    tiles.append(tile_at[lax.shift_right_logical(word, 10 * (u // 4)) & 1023])
                columns.append(jnp.concatenate(tiles, axis=0))
                blocks += [piece[i, u] for piece in pieces[:4]]
                blocks.append(pieces[4 + half][i - GROUP * half, u])
                blocks += [piece[i, u] for piece in pieces[6:]]
            picked = jnp.concatenate(columns, axis=1)
            total += jnp.dot(picked, jnp.concatenate(blocks, axis=0), preferred_element_type=jnp.float32)
        total = (total * scale).reshape(slots, width, size)
        if is_first:
            (out,) = outs
            out[i] = (-total).astype(out.dtype)
            line = lax.broadcasted_iota(jnp.int32, (width, size), 0)
            lane = lax.broadcasted_iota(jnp.int32, (width, size), 1)
            diagonal = jnp.where(lane == line + z * width, 3.0, 0.0)
            out[i, 0] = (diagonal - total[0]).astype(out.dtype)
        else:
            keep, send = outs
            to = i + offset
            low, high = total[:, :width // 2], total[:, width // 2:]
            keep[to] = jnp.where(core == 0, low, high).astype(keep.dtype)
            send[to] = jnp.where(core == 0, high, low).astype(send.dtype)
        return carry

    for half in range(2):
        lax.fori_loop(GROUP * half, GROUP * (half + 1), functools.partial(one_row, half), 0, unroll=GROUP)


def product(first_block, is_first, scale, index, parts, pieces, after=()):
    rows, slots, width, size = parts[0].shape
    dtype = parts[0].dtype
    if is_first:
        outs = jax.ShapeDtypeStruct((rows, slots, width, size), dtype)
        out_specs = pl.BlockSpec(memory_space=pltpu.VMEM)
    else:
        out_rows = 2 * rows if after else rows
        outs = [jax.ShapeDtypeStruct((out_rows, slots, width // 2, size), dtype)] * 2
        out_specs = [pl.BlockSpec(memory_space=pltpu.VMEM)] * 2
    flops = 2 * rows * slots * slots * width * size * size
    return pl.pallas_call(
        functools.partial(product_kernel, first_block, is_first, scale, len(after)),
        out_shape=outs,
        in_specs=[pl.BlockSpec(memory_space=pl.ANY)]
        + [pl.BlockSpec(memory_space=pltpu.VMEM)] * 12
        + [pl.BlockSpec(memory_space=pltpu.VMEM if len(after) == 2 else pl.ANY)] * len(after),
        out_specs=out_specs,
        scratch_shapes=[
            pltpu.VMEM((4 * rows + 1, 16, width, size), dtype),
            pltpu.SMEM(index.shape, index.dtype),
            pltpu.SemaphoreType.DMA,
        ],
        compiler_params=pltpu.CompilerParams(vmem_limit_bytes=8 * 2**20),
        cost_estimate=pl.CostEstimate(flops=COST * flops, bytes_accessed=rows * slots * size * size * 2, transcendentals=0),
    )(index, *parts, *pieces, *after)


def gather_ring(streams, ring):
    count = 2 * ring
    up = [(i, (i + 2) % count) for i in range(count)]
    down = [((i + 2) % count, i) for i in range(count)]
    risen = [[piece] for piece in streams]
    fallen = [[piece] for piece in streams]
    for step in range(ring // 2 - 1):
        for k in range(len(streams)):
            risen[k].append(lax.ppermute(risen[k][-1], "cols", up))
            fallen[k].append(lax.ppermute(fallen[k][-1], "cols", down))
    gathered = []
    for k in range(len(streams)):
        half = streams[k].shape[0] // 2
        last_up = lax.ppermute(risen[k][-1][:half], "cols", up)
        last_down = lax.ppermute(fallen[k][-1][half:], "cols", down)
        gathered.append(fallen[k] + [last_up, last_down] + risen[k][:0:-1])
    return gathered


def local(columns, fetch, values):
    rows_here, slots, half_width, size = values.shape
    cols = lax.axis_size("cols")
    count = lax.axis_size("rows")
    col = lax.axis_index("cols")
    core = col % 2
    first = core == 0
    swap = [(i, i ^ 1) for i in range(cols)]

    def outward(piece):
        pairs = []
        for r in range(count):
            for c in range(cols):
                to = ((r - 1) % count, c + 1) if c % 2 == 0 else ((r + 1) % count, c - 1)
                pairs.append((r * cols + c, to[0] * cols + to[1]))
        return lax.ppermute(piece, ("rows", "cols"), pairs)

    origin = lax.axis_index("rows") * rows_here + core * 16
    total = rows_here * count
    away = (columns - origin + total // 2) % total - total // 2 + 8
    part = jnp.where(first, away // 8, 3 - away // 8)
    place = (part * 8 + away % 8) * 16
    index = jnp.where(fetch >= 0, place[:, :, None] + fetch, 32 * 16).transpose(1, 2, 0)
    index = index[:4] + index[4:8] * 1024 + index[8:] * 1024**2

    other = lax.ppermute(values, "cols", swap)
    other, index = lax.optimization_barrier((other, index))

    def joined(number):
        start = jnp.where(first, 8 * number, 24 - 8 * number)
        mine = lax.dynamic_slice_in_dim(values, start, 8, 0)
        theirs = lax.dynamic_slice_in_dim(other, start, 8, 0)
        low = jnp.where(first, mine, theirs)
        high = jnp.where(first, theirs, mine)
        return jnp.concatenate([low, high], axis=2)

    outer_rows, inner_rows, beyond = joined(0), joined(1), joined(2)
    outer_halo = outward(outer_rows)
    outer_pieces, inner_pieces = gather_ring([outer_rows, inner_rows], cols // 2)

    scale = 1.0 / (slots * size)
    shifted_outer = product(0, True, scale, index, (outer_halo, outer_rows, inner_rows), outer_pieces)
    shifted_outward = outward(shifted_outer)
    shifted_inner = product(1, True, scale, index, (outer_rows, inner_rows, beyond), inner_pieces, [shifted_outer])
    shifted_beyond = lax.ppermute(shifted_inner, "cols", swap)
    parts = (shifted_outward, shifted_outer, shifted_inner)
    done_outer = product(0, False, 0.5, index, parts, outer_pieces)
    parts = (shifted_outer, shifted_inner, shifted_beyond)
    keep, send = product(1, False, 0.5, index, parts, inner_pieces, done_outer)
    got = lax.ppermute(send, "cols", swap)
    return jnp.where(first, jnp.concatenate([keep, got]), jnp.concatenate([got, keep]))


def solution(mesh):
    in_specs = (P("rows", None), P("rows", None, None), P("rows", None, "cols", None))
    out_specs = P("rows", None, "cols", None)
    return jax.shard_map(local, mesh=mesh, in_specs=in_specs, out_specs=out_specs, check_vma=False)
```

```python
import functools

import jax
import jax.numpy as jnp
from jax import lax
from jax.experimental import pallas as pl
from jax.experimental.pallas import tpu as pltpu
from jax.sharding import PartitionSpec as P

UNROLL = 8


def product_kernel(first_block, is_first, scale, extra, index_from, *refs):
    parts, pieces = refs[:3], refs[3:11]
    outs, (window, index_ref, index_sem) = refs[11 + extra:-3], refs[-3:]
    rows, slots, width, size = parts[0].shape
    col = lax.axis_index("cols")
    z, core = col // 2, lax.rem(col, 2)
    first_row = rows * jnp.where(core == 0, first_block, 3 - first_block)

    index_copy = pltpu.make_async_copy(index_from, index_ref, index_sem)
    index_copy.start()
    turn = lax.rem(size - width * z, size)
    for k, part in enumerate(parts):
        to = rows * (first_block + k) + (core if part.shape[0] < rows else 0)
        for row in range(part.shape[0]):
            window[to + row, pl.ds(0, slots)] = pltpu.roll(part[row], turn, 2)
    window[4 * rows, 0] = jnp.zeros((width, size), window.dtype)
    index_copy.wait()
    tile_at = window.reshape(window.shape[0] * window.shape[1], width, size)

    offset = 0
    if extra == 2:
        offset = rows * core
        for out, done in zip(outs, refs[11:13]):
            out[pl.ds(rows - offset, rows)] = done[...]

    def one_row(i, carry):
        total = jnp.zeros((slots * width, size), jnp.float32)
        for t in range(0, slots, 6):
            columns, blocks = [], []
            for u in range(t, t + 6):
                tiles = []
                for s in range(slots):
                    word = index_ref[u % 4, s, first_row + i]
                    tiles.append(tile_at[lax.shift_right_logical(word, 10 * (u // 4)) & 1023])
                columns.append(jnp.concatenate(tiles, axis=0))
                blocks += [piece[i, u] for piece in pieces]
            picked = jnp.concatenate(columns, axis=1)
            total += jnp.dot(picked, jnp.concatenate(blocks, axis=0), preferred_element_type=jnp.float32)
        total = (total * scale).reshape(slots, width, size)
        if is_first:
            out = outs[0]
            out[i] = (-total).astype(out.dtype)
            line = lax.broadcasted_iota(jnp.int32, (width, size), 0)
            lane = lax.broadcasted_iota(jnp.int32, (width, size), 1)
            diagonal = jnp.where(lane == line + z * width, 3.0, 0.0)
            out[i, 0] = (diagonal - total[0]).astype(out.dtype)
        else:
            keep, send = outs
            to = i + offset
            low, high = total[:, :width // 2], total[:, width // 2:]
            keep[to] = jnp.where(core == 0, low, high).astype(keep.dtype)
            send[to] = jnp.where(core == 0, high, low).astype(send.dtype)
        return carry

    lax.fori_loop(0, rows, one_row, 0, unroll=UNROLL)
    if is_first and first_block == 1:
        outs[1][...] = outs[0][pl.ds(1 - core, rows - 1)]


def product(first_block, is_first, scale, index, parts, pieces, after=(), cost=10):
    rows, slots, width, size = parts[0].shape
    dtype = parts[0].dtype
    if is_first:
        outs = [jax.ShapeDtypeStruct((rows - k, slots, width, size), dtype) for k in range(1 + first_block)]
        out_specs = [pl.BlockSpec(memory_space=pltpu.VMEM)] * (1 + first_block)
    else:
        out_rows = 2 * rows if after else rows
        outs = [jax.ShapeDtypeStruct((out_rows, slots, width // 2, size), dtype)] * 2
        out_specs = [pl.BlockSpec(memory_space=pltpu.VMEM)] * 2
    flops = 2 * rows * slots * slots * width * size * size
    return pl.pallas_call(
        functools.partial(product_kernel, first_block, is_first, scale, len(after)),
        out_shape=outs,
        in_specs=[pl.BlockSpec(memory_space=pl.ANY)]
        + [pl.BlockSpec(memory_space=pltpu.VMEM)] * 11
        + [pl.BlockSpec(memory_space=pltpu.VMEM if len(after) == 2 else pl.ANY)] * len(after),
        out_specs=out_specs,
        scratch_shapes=[
            pltpu.VMEM((4 * rows + 1, 16, width, size), dtype),
            pltpu.SMEM(index.shape, index.dtype),
            pltpu.SemaphoreType.DMA,
        ],
        compiler_params=pltpu.CompilerParams(vmem_limit_bytes=8 * 2**20),
        cost_estimate=pl.CostEstimate(flops=int(cost * flops), bytes_accessed=rows * slots * size * size * 2, transcendentals=0),
    )(index, *parts, *pieces, *after)


def gather_ring(streams, ring):
    count = 2 * ring
    up = [(i, (i + 2) % count) for i in range(count)]
    down = [((i + 2) % count, i) for i in range(count)]
    risen = [[piece] for piece in streams]
    fallen = [[piece] for piece in streams]
    for step in range(ring // 2 - 1):
        for k in range(len(streams)):
            risen[k].append(lax.ppermute(risen[k][-1], "cols", up))
            fallen[k].append(lax.ppermute(fallen[k][-1], "cols", down))
    first = lax.axis_index("cols") % 2 == 0
    outward = [(i, (i + 2) % count if i % 2 == 0 else (i - 2) % count) for i in range(count)]
    gathered = []
    for k in range(len(streams)):
        farthest = lax.ppermute(jnp.where(first, risen[k][-1], fallen[k][-1]), "cols", outward)
        gathered.append(fallen[k] + [farthest] + risen[k][:0:-1])
    return gathered


def local(columns, fetch, values):
    rows_here, slots, half_width, size = values.shape
    cols = lax.axis_size("cols")
    count = lax.axis_size("rows")
    col = lax.axis_index("cols")
    core = col % 2
    first = core == 0
    swap = [(i, i ^ 1) for i in range(cols)]

    def outward(piece):
        pairs = []
        for r in range(count):
            for c in range(cols):
                to = ((r - 1) % count, c + 1) if c % 2 == 0 else ((r + 1) % count, c - 1)
                pairs.append((r * cols + c, to[0] * cols + to[1]))
        return lax.ppermute(piece, ("rows", "cols"), pairs)

    origin = lax.axis_index("rows") * rows_here + core * 16
    total = rows_here * count
    away = (columns - origin + total // 2) % total - total // 2 + 8
    part = jnp.where(first, away // 8, 3 - away // 8)
    place = (part * 8 + away % 8) * 16
    index = jnp.where(fetch >= 0, place[:, :, None] + fetch, 32 * 16).transpose(1, 2, 0)
    index = index[:4] + index[4:8] * 1024 + index[8:] * 1024**2

    other = lax.ppermute(values, "cols", swap)
    other, index = lax.optimization_barrier((other, index))

    def joined(number):
        start = jnp.where(first, 8 * number, 24 - 8 * number)
        mine = lax.dynamic_slice_in_dim(values, start, 8, 0)
        theirs = lax.dynamic_slice_in_dim(other, start, 8, 0)
        low = jnp.where(first, mine, theirs)
        high = jnp.where(first, theirs, mine)
        return jnp.concatenate([low, high], axis=2)

    outer_rows, inner_rows, beyond = joined(0), joined(1), joined(2)
    outer_halo = outward(outer_rows)
    outer_pieces, inner_pieces = gather_ring([outer_rows, inner_rows], cols // 2)

    scale = 1.0 / (slots * size)
    (shifted_outer,) = product(0, True, scale, index, (outer_halo, outer_rows, inner_rows), outer_pieces)
    shifted_outward = outward(shifted_outer)
    shifted_inner, inner_edge = product(1, True, scale, index, (outer_rows, inner_rows, beyond), inner_pieces, [shifted_outer])
    shifted_beyond = lax.ppermute(inner_edge, "cols", swap)
    parts = (shifted_outer, shifted_inner, shifted_beyond)
    done_inner = product(1, False, 0.5, index, parts, inner_pieces, cost=0.01)
    parts = (shifted_outward, shifted_outer, shifted_inner)
    keep, send = product(0, False, 0.5, index, parts, outer_pieces, done_inner)
    got = lax.ppermute(send, "cols", swap)
    return jnp.where(first, jnp.concatenate([keep, got]), jnp.concatenate([got, keep]))


def solution(mesh):
    in_specs = (P("rows", None), P("rows", None, None), P("rows", None, "cols", None))
    out_specs = P("rows", None, "cols", None)
    return jax.shard_map(local, mesh=mesh, in_specs=in_specs, out_specs=out_specs, check_vma=False)
```

```python
import functools

import jax
import jax.numpy as jnp
from jax import lax
from jax.experimental import pallas as pl
from jax.experimental.pallas import tpu as pltpu
from jax.sharding import PartitionSpec as P

UNROLL = 8


def product_kernel(first_block, is_first, scale, extra, index_from, *refs):
    parts, pieces = refs[:3], refs[3:11]
    outs, (window, index_ref, index_sem) = refs[11 + extra:-3], refs[-3:]
    rows, slots, width, size = parts[0].shape
    ring = size // width
    col = lax.axis_index("cols")
    z, core = col // 2, lax.rem(col, 2)
    first_row = rows * jnp.where(core == 0, first_block, 3 - first_block)

    index_copy = pltpu.make_async_copy(index_from, index_ref, index_sem)
    index_copy.start()
    lane = lax.broadcasted_iota(jnp.int32, (size, size), 1)
    away = jnp.where(core == 0, z + lane // width, z - lane // width + ring) & (ring - 1)
    turned = lax.broadcasted_iota(jnp.int32, (size, size), 0) == away * width + (lane & (width - 1))
    turned = turned.astype(jnp.float32).astype(window.dtype)
    for k, part in enumerate(parts):
        to = rows * (first_block + k) + (core if part.shape[0] < rows else 0)
        for row in range(part.shape[0]):
            lines = jnp.dot(part[row].reshape(slots * width, size), turned, preferred_element_type=jnp.float32)
            window[to + row, pl.ds(0, slots)] = lines.astype(window.dtype).reshape(slots, width, size)
    window[4 * rows, 0] = jnp.zeros((width, size), window.dtype)
    index_copy.wait()
    tile_at = window.reshape(window.shape[0] * window.shape[1], width, size)

    offset = 0
    if extra == 2:
        offset = rows * core
        for out, done in zip(outs, refs[11:13]):
            out[pl.ds(rows - offset, rows)] = done[...]

    def one_row(i, carry):
        total = jnp.zeros((slots * width, size), jnp.float32)
        for t in range(0, slots, 6):
            columns, blocks = [], []
            for u in range(t, t + 6):
                tiles = []
                for s in range(slots):
                    word = index_ref[u % 4, s, first_row + i]
                    tiles.append(tile_at[lax.shift_right_logical(word, 10 * (u // 4)) & 1023])
                columns.append(jnp.concatenate(tiles, axis=0))
                blocks += [piece[i, u] for piece in pieces]
            picked = jnp.concatenate(columns, axis=1)
            total += jnp.dot(picked, jnp.concatenate(blocks, axis=0), preferred_element_type=jnp.float32)
        total = (total * scale).reshape(slots, width, size)
        if is_first:
            out = outs[0]
            out[i] = (-total).astype(out.dtype)
            line = lax.broadcasted_iota(jnp.int32, (width, size), 0)
            lane = lax.broadcasted_iota(jnp.int32, (width, size), 1)
            diagonal = jnp.where(lane == line + z * width, 3.0, 0.0)
            out[i, 0] = (diagonal - total[0]).astype(out.dtype)
        else:
            keep, send = outs
            to = i + offset
            low, high = total[:, :width // 2], total[:, width // 2:]
            keep[to] = jnp.where(core == 0, low, high).astype(keep.dtype)
            send[to] = jnp.where(core == 0, high, low).astype(send.dtype)
        return carry

    lax.fori_loop(0, rows, one_row, 0, unroll=UNROLL)
    if is_first and first_block == 1:
        outs[1][...] = outs[0][pl.ds(1 - core, rows - 1)]


def product(first_block, is_first, scale, index, parts, pieces, after=(), cost=10):
    rows, slots, width, size = parts[0].shape
    dtype = parts[0].dtype
    if is_first:
        outs = [jax.ShapeDtypeStruct((rows - k, slots, width, size), dtype) for k in range(1 + first_block)]
        out_specs = [pl.BlockSpec(memory_space=pltpu.VMEM)] * (1 + first_block)
    else:
        out_rows = 2 * rows if after else rows
        outs = [jax.ShapeDtypeStruct((out_rows, slots, width // 2, size), dtype)] * 2
        out_specs = [pl.BlockSpec(memory_space=pltpu.VMEM)] * 2
    flops = 2 * rows * slots * slots * width * size * size
    return pl.pallas_call(
        functools.partial(product_kernel, first_block, is_first, scale, len(after)),
        out_shape=outs,
        in_specs=[pl.BlockSpec(memory_space=pl.ANY)]
        + [pl.BlockSpec(memory_space=pltpu.VMEM)] * 11
        + [pl.BlockSpec(memory_space=pltpu.VMEM if len(after) == 2 else pl.ANY)] * len(after),
        out_specs=out_specs,
        scratch_shapes=[
            pltpu.VMEM((4 * rows + 1, 16, width, size), dtype),
            pltpu.SMEM(index.shape, index.dtype),
            pltpu.SemaphoreType.DMA,
        ],
        compiler_params=pltpu.CompilerParams(vmem_limit_bytes=8 * 2**20),
        cost_estimate=pl.CostEstimate(flops=int(cost * flops), bytes_accessed=rows * slots * size * size * 2, transcendentals=0),
    )(index, *parts, *pieces, *after)


def gather_ring(streams, ring):
    count = 2 * ring
    ahead = [(i, (i + 2) % count if i % 2 == 0 else (i - 2) % count) for i in range(count)]
    back = [(to, i) for i, to in ahead]
    gone = [[piece] for piece in streams]
    come = [[piece] for piece in streams]
    for step in range(ring // 2 - 1):
        for k in range(len(streams)):
            gone[k].append(lax.ppermute(gone[k][-1], "cols", ahead))
            come[k].append(lax.ppermute(come[k][-1], "cols", back))
    return [come[k] + [lax.ppermute(gone[k][-1], "cols", ahead)] + gone[k][:0:-1] for k in range(len(streams))]


def local(columns, fetch, values):
    rows_here, slots, half_width, size = values.shape
    cols = lax.axis_size("cols")
    count = lax.axis_size("rows")
    col = lax.axis_index("cols")
    core = col % 2
    first = core == 0
    swap = [(i, i ^ 1) for i in range(cols)]

    def outward(piece):
        pairs = []
        for r in range(count):
            for c in range(cols):
                to = ((r - 1) % count, c + 1) if c % 2 == 0 else ((r + 1) % count, c - 1)
                pairs.append((r * cols + c, to[0] * cols + to[1]))
        return lax.ppermute(piece, ("rows", "cols"), pairs)

    origin = lax.axis_index("rows") * rows_here + core * 16
    total = rows_here * count
    away = (columns - origin + total // 2) % total - total // 2 + 8
    part = jnp.where(first, away // 8, 3 - away // 8)
    place = (part * 8 + away % 8) * 16
    index = jnp.where(fetch >= 0, place[:, :, None] + fetch, 32 * 16).transpose(1, 2, 0)
    index = index[:4] + index[4:8] * 1024 + index[8:] * 1024**2

    other = lax.ppermute(values, "cols", swap)
    other, index = lax.optimization_barrier((other, index))

    def joined(number):
        start = jnp.where(first, 8 * number, 24 - 8 * number)
        mine = lax.dynamic_slice_in_dim(values, start, 8, 0)
        theirs = lax.dynamic_slice_in_dim(other, start, 8, 0)
        low = jnp.where(first, mine, theirs)
        high = jnp.where(first, theirs, mine)
        return jnp.concatenate([low, high], axis=2)

    outer_rows, inner_rows, beyond = joined(0), joined(1), joined(2)
    outer_halo = outward(outer_rows)
    outer_pieces, inner_pieces = gather_ring([outer_rows, inner_rows], cols // 2)

    scale = 1.0 / (slots * size)
    (shifted_outer,) = product(0, True, scale, index, (outer_halo, outer_rows, inner_rows), outer_pieces)
    shifted_outward = outward(shifted_outer)
    shifted_inner, inner_edge = product(1, True, scale, index, (outer_rows, inner_rows, beyond), inner_pieces, [shifted_outer])
    shifted_beyond = lax.ppermute(inner_edge, "cols", swap)
    parts = (shifted_outer, shifted_inner, shifted_beyond)
    done_inner = product(1, False, 0.5, index, parts, inner_pieces, cost=0.01)
    parts = (shifted_outward, shifted_outer, shifted_inner)
    keep, send = product(0, False, 0.5, index, parts, outer_pieces, done_inner)
    got = lax.ppermute(send, "cols", swap)
    return jnp.where(first, jnp.concatenate([keep, got]), jnp.concatenate([got, keep]))


def solution(mesh):
    in_specs = (P("rows", None), P("rows", None, None), P("rows", None, "cols", None))
    out_specs = P("rows", None, "cols", None)
    return jax.shard_map(local, mesh=mesh, in_specs=in_specs, out_specs=out_specs, check_vma=False)
```

```python
import functools

import jax
import jax.numpy as jnp
from jax import lax
from jax.experimental import pallas as pl
from jax.experimental.pallas import tpu as pltpu
from jax.sharding import PartitionSpec as P

UNROLL = 8


def product_kernel(first_block, is_first, scale, extra, index_from, *refs):
    parts, pieces = refs[:3], refs[3:11]
    outs, (window, index_ref, index_sem) = refs[11 + extra:-3], refs[-3:]
    rows, slots, width, size = parts[0].shape
    ring = size // width
    col = lax.axis_index("cols")
    z, core = col // 2, lax.rem(col, 2)
    first_row = rows * jnp.where(core == 0, first_block, 3 - first_block)

    index_copy = pltpu.make_async_copy(index_from, index_ref, index_sem)
    index_copy.start()
    lane = lax.broadcasted_iota(jnp.int32, (size, size), 1)
    away = jnp.where(core == 0, z + lane // width, z - lane // width + ring) & (ring - 1)
    turned = lax.broadcasted_iota(jnp.int32, (size, size), 0) == away * width + (lane & (width - 1))
    turned = turned.astype(jnp.float32).astype(window.dtype)
    for k, part in enumerate(parts):
        to = rows * (first_block + k) + (core if part.shape[0] < rows else 0)
        for row in range(part.shape[0]):
            lines = jnp.dot(part[row].reshape(slots * width, size), turned, preferred_element_type=jnp.float32)
            window[to + row, pl.ds(0, slots)] = lines.astype(window.dtype).reshape(slots, width, size)
    window[4 * rows, 0] = jnp.zeros((width, size), window.dtype)
    index_copy.wait()
    tile_at = window.reshape(window.shape[0] * window.shape[1], width, size)

    offset = 0
    if extra == 2:
        offset = rows * core
        for out, done in zip(outs, refs[11:13]):
            out[pl.ds(rows - offset, rows)] = done[...]

    def one_row(i, carry):
        total = jnp.zeros((slots * width, size), jnp.float32)
        for t in range(0, slots, 6):
            columns, blocks = [], []
            for u in range(t, t + 6):
                tiles = []
                for s in range(slots):
                    word = index_ref[s, 4 * rows * (u % 4) + first_row + i]
                    place = (word & 1023, lax.shift_right_logical(word, 10) & 1023, lax.shift_right_logical(word, 20))[u // 4]
                    tiles.append(tile_at[place])
                columns.append(jnp.concatenate(tiles, axis=0))
                blocks += [piece[i, u] for piece in pieces]
            picked = jnp.concatenate(columns, axis=1)
            total += jnp.dot(picked, jnp.concatenate(blocks, axis=0), preferred_element_type=jnp.float32)
        total = (total * scale).reshape(slots, width, size)
        if is_first:
            out = outs[0]
            out[i] = (-total).astype(out.dtype)
            line = lax.broadcasted_iota(jnp.int32, (width, size), 0)
            lane = lax.broadcasted_iota(jnp.int32, (width, size), 1)
            diagonal = jnp.where(lane == line + z * width, 3.0, 0.0)
            out[i, 0] = (diagonal - total[0]).astype(out.dtype)
        else:
            keep, send = outs
            to = i + offset
            low, high = total[:, :width // 2], total[:, width // 2:]
            keep[to] = jnp.where(core == 0, low, high).astype(keep.dtype)
            send[to] = jnp.where(core == 0, high, low).astype(send.dtype)
        return carry

    lax.fori_loop(0, rows, one_row, 0, unroll=UNROLL)
    if is_first and first_block == 1:
        outs[1][...] = outs[0][pl.ds(1 - core, rows - 1)]


def product(first_block, is_first, scale, index, parts, pieces, after=(), cost=10):
    rows, slots, width, size = parts[0].shape
    dtype = parts[0].dtype
    if is_first:
        outs = [jax.ShapeDtypeStruct((rows - k, slots, width, size), dtype) for k in range(1 + first_block)]
        out_specs = [pl.BlockSpec(memory_space=pltpu.VMEM)] * (1 + first_block)
    else:
        out_rows = 2 * rows if after else rows
        outs = [jax.ShapeDtypeStruct((out_rows, slots, width // 2, size), dtype)] * 2
        out_specs = [pl.BlockSpec(memory_space=pltpu.VMEM)] * 2
    flops = 2 * rows * slots * slots * width * size * size
    return pl.pallas_call(
        functools.partial(product_kernel, first_block, is_first, scale, len(after)),
        out_shape=outs,
        in_specs=[pl.BlockSpec(memory_space=pl.ANY)]
        + [pl.BlockSpec(memory_space=pltpu.VMEM)] * 11
        + [pl.BlockSpec(memory_space=pltpu.VMEM if len(after) == 2 else pl.ANY)] * len(after),
        out_specs=out_specs,
        scratch_shapes=[
            pltpu.VMEM((4 * rows + 1, 16, width, size), dtype),
            pltpu.SMEM(index.shape, index.dtype),
            pltpu.SemaphoreType.DMA,
        ],
        compiler_params=pltpu.CompilerParams(vmem_limit_bytes=8 * 2**20),
        cost_estimate=pl.CostEstimate(flops=int(cost * flops), bytes_accessed=rows * slots * size * size * 2, transcendentals=0),
    )(index, *parts, *pieces, *after)


def gather_ring(streams, ring):
    count = 2 * ring
    ahead = [(i, (i + 2) % count if i % 2 == 0 else (i - 2) % count) for i in range(count)]
    back = [(to, i) for i, to in ahead]
    gone = [[piece] for piece in streams]
    come = [[piece] for piece in streams]
    for step in range(ring // 2 - 1):
        for k in range(len(streams)):
            gone[k].append(lax.ppermute(gone[k][-1], "cols", ahead))
            come[k].append(lax.ppermute(come[k][-1], "cols", back))
    return [come[k] + [lax.ppermute(gone[k][-1], "cols", ahead)] + gone[k][:0:-1] for k in range(len(streams))]


def local(columns, fetch, values):
    rows_here, slots, half_width, size = values.shape
    cols = lax.axis_size("cols")
    count = lax.axis_size("rows")
    col = lax.axis_index("cols")
    core = col % 2
    first = core == 0
    swap = [(i, i ^ 1) for i in range(cols)]

    def outward(piece):
        pairs = []
        for r in range(count):
            for c in range(cols):
                to = ((r - 1) % count, c + 1) if c % 2 == 0 else ((r + 1) % count, c - 1)
                pairs.append((r * cols + c, to[0] * cols + to[1]))
        return lax.ppermute(piece, ("rows", "cols"), pairs)

    origin = lax.axis_index("rows") * rows_here + core * 16
    total = rows_here * count
    away = (columns - origin + total // 2) % total - total // 2 + 8
    part = jnp.where(first, away // 8, 3 - away // 8)
    place = (part * 8 + away % 8) * 16
    index = jnp.where(fetch >= 0, place[:, :, None] + fetch, 32 * 16).transpose(1, 2, 0)
    index = index[:4] + index[4:8] * 1024 + index[8:] * 1024**2
    index = jnp.concatenate([index[k] for k in range(4)], axis=1)

    other = lax.ppermute(values, "cols", swap)
    other, index = lax.optimization_barrier((other, index))

    def joined(number):
        start = jnp.where(first, 8 * number, 24 - 8 * number)
        mine = lax.dynamic_slice_in_dim(values, start, 8, 0)
        theirs = lax.dynamic_slice_in_dim(other, start, 8, 0)
        low = jnp.where(first, mine, theirs)
        high = jnp.where(first, theirs, mine)
        return jnp.concatenate([low, high], axis=2)

    outer_rows, inner_rows, beyond = joined(0), joined(1), joined(2)
    outer_halo = outward(outer_rows)
    outer_pieces, inner_pieces = gather_ring([outer_rows, inner_rows], cols // 2)

    scale = 1.0 / (slots * size)
    (shifted_outer,) = product(0, True, scale, index, (outer_halo, outer_rows, inner_rows), outer_pieces)
    shifted_outward = outward(shifted_outer)
    shifted_inner, inner_edge = product(1, True, scale, index, (outer_rows, inner_rows, beyond), inner_pieces, [shifted_outer])
    shifted_beyond = lax.ppermute(inner_edge, "cols", swap)
    parts = (shifted_outer, shifted_inner, shifted_beyond)
    done_inner = product(1, False, 0.5, index, parts, inner_pieces, cost=0.01)
    parts = (shifted_outward, shifted_outer, shifted_inner)
    keep, send = product(0, False, 0.5, index, parts, outer_pieces, done_inner)
    got = lax.ppermute(send, "cols", swap)
    return jnp.where(first, jnp.concatenate([keep, got]), jnp.concatenate([got, keep]))


def solution(mesh):
    in_specs = (P("rows", None), P("rows", None, None), P("rows", None, "cols", None))
    out_specs = P("rows", None, "cols", None)
    return jax.shard_map(local, mesh=mesh, in_specs=in_specs, out_specs=out_specs, check_vma=False)
```
